128 devices in a mesh: row: 8 (over x, z_lo), col: 16 (over z_hi, y, core).
Axes of the slice: x: 4, y: 4, z: 4 (z_hi: 2, z_lo: 2; z = z_hi * 2 + z_lo), core: 2. Of those that a mesh axis runs over, the one named last changes fastest.
Arguments:
- act_q: bfloat16 [1024, 8192], P('col', 'row'), may hold values from -6 to 6
- act_scale: float32 [1024, 64], P('col', 'row'), may hold values from 0.25 to 4
- grad_q: bfloat16 [1024, 8192], P('col', 'row'), may hold values from -6 to 6
- grad_scale: float32 [1024, 64], P('col', 'row'), may hold values from 0.25 to 4
- gate_pre: bfloat16 [1024, 28672], P('row', 'col'), may hold values from -6 to 6
- up_pre: bfloat16 [1024, 28672], P('row', 'col'), may hold values from -6 to 6
- gate_weight: bfloat16 [8192, 28672], P('row', 'col'), may hold values from -0.0625 to 0.0625
- up_weight: bfloat16 [8192, 28672], P('row', 'col'), may hold values from -0.0625 to 0.0625
- down_weight: bfloat16 [28672, 8192], P('col', 'row'), may hold values from -0.03125 to 0.03125
Outputs:
- act_grad: bfloat16 [1024, 8192], P('col', 'row')
- gate_grad: bfloat16 [8192, 28672], P('row', 'col')
- up_grad: bfloat16 [8192, 28672], P('row', 'col')
- down_grad: bfloat16 [28672, 8192], P('col', 'row')
The draws below stay inside these ranges and needn't reach their ends.
All inputs are finite; a program needn't handle non-finite values.
Results may differ from the reference program's by a relative error of at most 0.027.
Values may be sent and summed in bfloat16 or wider, within the bound.
A program may use at most 128 MiB of HBM per device.

```python
import math
import jax
import jax.numpy as jnp

D = 8192
FF = 28672
BLOCK = 128
TOKENS = 1024


def block_scale(key, dims, pieces, smallest, top_value):
    loudness, own = 1.0, jax.random.fold_in(key, 6)
    for position, shards_of in pieces:
        draws = jnp.exp(jax.random.uniform(jax.random.fold_in(own, position), (shards_of,), jnp.float32, smallest / len(pieces), top_value / len(pieces)))
        loudness = loudness * jnp.repeat(draws, dims[position] // shards_of).reshape([-1 if axis == position else 1 for axis in range(len(dims))])
    return loudness


def gaussian(stream_key, extent, scale, most, cuts=(), kind=jnp.bfloat16):
    level = block_scale(stream_key, extent, cuts, -0.22, 0.18) if cuts else 1.0
    entries = jax.random.normal(stream_key, extent, jnp.float32) * scale * level
    return jnp.minimum(jnp.maximum(entries, -most), most).astype(kind)


def setup_inputs(seed: int = 0) -> dict:
    seeds = jax.random.split(jax.random.key(seed), 10)
    act_q = gaussian(seeds[0], (TOKENS, D), 1.0, 6.0, ((0, 16), (1, 8)))
    act_scale = jnp.clip(jnp.exp(math.log(4.0) - 2.7725887 * jax.random.uniform(seeds[1], (TOKENS, D // BLOCK), jnp.float32) ** block_scale(seeds[1], (TOKENS, D // BLOCK), ((0, 16), (1, 8)), -0.2, 0.2)), 0.25, 4.0)
    grad_q = gaussian(seeds[2], (TOKENS, D), 1.0, 6.0, ((0, 16), (1, 8)))
    grad_scale = jnp.clip(jnp.exp(math.log(4.0) - 2.7725887 * jax.random.uniform(seeds[3], (TOKENS, D // BLOCK), jnp.float32) ** block_scale(seeds[3], (TOKENS, D // BLOCK), ((0, 16), (1, 8)), -0.2, 0.2)), 0.25, 4.0)
    gate_pre = gaussian(seeds[4], (TOKENS, FF), 1.0, 6.0, ((0, 8), (1, 16)))
    up_pre = gaussian(seeds[5], (TOKENS, FF), 1.0, 6.0, ((0, 8), (1, 16)))
    gate_weight = gaussian(seeds[6], (D, FF), D ** -0.5, 0.0625, ((0, 8), (1, 16)))
    up_weight = gaussian(seeds[7], (D, FF), D ** -0.5, 0.0625, ((0, 8), (1, 16)))
    down_weight = gaussian(seeds[8], (FF, D), FF ** -0.5, 0.03125, ((0, 16), (1, 8)))
    return {"act_q": act_q, "act_scale": act_scale, "grad_q": grad_q, "grad_scale": grad_scale, "gate_pre": gate_pre, "up_pre": up_pre, "gate_weight": gate_weight, "up_weight": up_weight, "down_weight": down_weight}


def dequant(values, scales):
    tok, width = values.shape
    blocks = values.astype(jnp.float32).reshape(tok, width // 128, 128) * scales[:, :, None]
    return blocks.reshape(tok, width).astype(jnp.bfloat16)


def reference(act_q, act_scale, grad_q, grad_scale, gate_pre, up_pre, gate_weight, up_weight, down_weight):
    inputs = dequant(act_q, act_scale)
    out_grad = dequant(grad_q, grad_scale)
    hidden_grad = jnp.dot(out_grad, down_weight.T, preferred_element_type=jnp.float32)
    gate_val = gate_pre.astype(jnp.float32)
    up_val = up_pre.astype(jnp.float32)
    sigmoid_gate = jax.nn.sigmoid(gate_val)
    hidden = (gate_val * sigmoid_gate * up_val).astype(jnp.bfloat16)
    gate_delta = (hidden_grad * up_val * sigmoid_gate * (1.0 + gate_val * (1.0 - sigmoid_gate))).astype(jnp.bfloat16)
    up_delta = (hidden_grad * gate_val * sigmoid_gate).astype(jnp.bfloat16)
    factor = 1.0 / (TOKENS ** 0.5)
    down_grad = (jnp.dot(hidden.T, out_grad, preferred_element_type=jnp.float32) * factor).astype(jnp.bfloat16)
    gate_grad = (jnp.dot(inputs.T, gate_delta, preferred_element_type=jnp.float32) * factor).astype(jnp.bfloat16)
    up_grad = (jnp.dot(inputs.T, up_delta, preferred_element_type=jnp.float32) * factor).astype(jnp.bfloat16)
    act_grad = jnp.dot(gate_delta, gate_weight.T, preferred_element_type=jnp.float32)
    act_grad = act_grad + jnp.dot(up_delta, up_weight.T, preferred_element_type=jnp.float32)
    return act_grad.astype(jnp.bfloat16), gate_grad, up_grad, down_grad
```

```python
import math

import jax
import jax.numpy as jnp
from jax import lax
from jax.experimental import pallas as pl
from jax.experimental.pallas import tpu as pltpu
from jax.sharding import PartitionSpec as P

MESH = pl.DeviceIdType.MESH
T, DB, FB = 1024, 1024, 1792
PR = 80
QR = 128 - PR
PA, QA = 48, 32
PB, QB = PR - PA, QR - QA
F32, BF16 = jnp.float32, jnp.bfloat16

N_SEMS = 3 * 16 + 15 + 2 * 17 + 21


def nt(a, b):
    return lax.dot_general(a, b, (((1,), (1,)), ((), ())), preferred_element_type=F32)


def rows(ref, start, n):
    return ref.at[pl.ds(pl.multiple_of(start, 16), n), :]


def kernel(
    act_q, act_scale, grad_q, grad_scale, gate_pre, up_pre, gate_w, up_w, down_w,
    act_grad, inputs_out, out_grad_out, hidden_out, gate_out, up_out,
    g_all, u_all, h_all, part, landed, og_all, in_all, dw, gw, uw,
    hid, gd, ud, act_part, sib_in, y_out, y_in, z_out, z_in, final,
    send_sems, recv_sems, local_sems,
):
    row, col = lax.axis_index("row"), lax.axis_index("col")
    x, z = lax.div(row, 2), lax.rem(row, 2)
    zh, y, core = lax.div(col, 8), lax.rem(lax.div(col, 2), 4), lax.rem(col, 2)
    xl, xr, xf = lax.rem(x + 3, 4), lax.rem(x + 1, 4), lax.rem(x + 2, 4)
    yl, yr, yf = lax.rem(y + 3, 4), lax.rem(y + 1, 4), lax.rem(y + 2, 4)
    oz, ozh, ocore = 1 - z, 1 - zh, 1 - core

    def rdev(xx, zz):
        return (xx * 2 + zz, col)

    def cidx(hh, yy, cc):
        return hh * 8 + yy * 2 + cc

    def cdev(hh, yy, cc):
        return (row, cidx(hh, yy, cc))

    zdev, ldev, rtdev = rdev(x, oz), rdev(xl, z), rdev(xr, z)
    hdev, yldev, yrdev, yfdev = cdev(ozh, y, core), cdev(zh, yl, core), cdev(zh, yr, core), cdev(zh, yf, core)
    sdev = cdev(zh, y, ocore)

    count = [0]
    pending = []

    def make(src, dst, dev):
        i = count[0]
        count[0] += 1
        return pltpu.make_async_remote_copy(
            src_ref=src, dst_ref=dst, send_sem=send_sems.at[i], recv_sem=recv_sems.at[i],
            device_id=dev, device_id_type=MESH,
        )

    def send(src, dst, dev):
        copy = make(src, dst, dev)
        copy.start()
        pending.append(copy)
        return copy

    local_count = [0]

    def local(src, dst):
        copy = pltpu.make_async_copy(src, dst, local_sems.at[local_count[0]])
        local_count[0] += 1
        copy.start()
        return copy

    g_load = local(gate_pre, rows(g_all, row * 128, 128))
    u_load = local(up_pre, rows(u_all, row * 128, 128))
    dw_load = local(down_w, dw)
    gw_load = local(gate_w, gw)
    uw_load = local(up_w, uw)

    for blk in range(8):
        lanes = pl.ds(blk * 128, 128)
        og_all[pl.ds(pl.multiple_of(col * 64, 64), 64), lanes] = (
            grad_q[:, lanes].astype(F32) * grad_scale[:, blk : blk + 1]
        ).astype(BF16)
        in_all[pl.ds(pl.multiple_of(col * 64, 64), 64), lanes] = (
            act_q[:, lanes].astype(F32) * act_scale[:, blk : blk + 1]
        ).astype(BF16)

    barrier = pltpu.get_barrier_semaphore()
    partners = (zdev, ldev, rtdev, hdev, yldev, yrdev, yfdev, sdev)
    for dev in partners:
        pl.semaphore_signal(barrier, inc=1, device_id=dev, device_id_type=MESH)
    pl.semaphore_wait(barrier, len(partners))

    def ctile(ref, hh, yy, cc, off=0, n=64):
        return rows(ref, cidx(hh, yy, cc) * 64 + off, n)

    def csend(ref, hh, yy, cc, dev, off=0, n=64):
        where = ctile(ref, hh, yy, cc, off, n)
        return send(where, where, dev)

    def col_own(ref):
        return dict(
            h=csend(ref, zh, y, core, hdev),
            r=csend(ref, zh, y, core, yrdev),
            l=csend(ref, zh, y, core, yldev),
            s=[csend(ref, zh, y, core, sdev)],
        )

    def col_mid(ref, c):
        c["h"].wait_recv()
        c["hr"] = csend(ref, ozh, y, core, yrdev)
        c["hl"] = csend(ref, ozh, y, core, yldev)
        c["s"].append(csend(ref, ozh, y, core, sdev))
        c["r"].wait_recv()
        c["fr"] = csend(ref, zh, yl, core, yrdev, 0, 32)
        c["s"].append(csend(ref, zh, yl, core, sdev))
        c["l"].wait_recv()
        c["fl"] = csend(ref, zh, yr, core, yldev, 32, 32)
        c["s"].append(csend(ref, zh, yr, core, sdev))

    def col_late(ref, c):
        c["hr"].wait_recv()
        c["hfr"] = csend(ref, ozh, yl, core, yrdev, 0, 32)
        c["s"].append(csend(ref, ozh, yl, core, sdev))
        c["hl"].wait_recv()
        c["hfl"] = csend(ref, ozh, yr, core, yldev, 32, 32)
        c["s"].append(csend(ref, ozh, yr, core, sdev))
        c["fr"].wait_recv()
        c["fl"].wait_recv()
        c["s"].append(csend(ref, zh, yf, core, sdev))
        c["hfr"].wait_recv()
        c["hfl"].wait_recv()
        c["s"].append(csend(ref, ozh, yf, core, sdev))

    def col_end(c):
        for copy in c["s"]:
            copy.wait_recv()

    def rsend(ref, xx, zz, off, n, dev):
        where = rows(ref, (xx * 2 + zz) * 128 + off, n)
        return send(where, where, dev)

    def row_own(ref):
        return dict(
            zp=rsend(ref, x, z, 0, PR, zdev),
            r=rsend(ref, x, z, 0, 128, rtdev),
            l=rsend(ref, x, z, 0, 128, ldev),
            zq=rsend(ref, x, z, PR, QR, zdev),
        )

    def row_mid(ref, c):
        c["zp"].wait_recv()
        c["pr"] = rsend(ref, x, oz, 0, PR, rtdev)
        c["pl"] = rsend(ref, x, oz, 0, PR, ldev)
        c["r"].wait_recv()
        c["fqr"] = rsend(ref, xl, z, PR + QA, QB, rtdev)
        c["zql"] = rsend(ref, xl, z, PR, QR, zdev)
        c["fpr"] = rsend(ref, xl, z, 0, PA, rtdev)
        c["l"].wait_recv()
        c["fql"] = rsend(ref, xr, z, PR, QA, ldev)
        c["zqr"] = rsend(ref, xr, z, PR, QR, zdev)
        c["fpl"] = rsend(ref, xr, z, PA, PB, ldev)

    def row_late(ref, c):
        c["pr"].wait_recv()
        c["gpr"] = rsend(ref, xl, oz, 0, PA, rtdev)
        c["pl"].wait_recv()
        c["gpl"] = rsend(ref, xr, oz, PA, PB, ldev)
        c["fqr"].wait_recv()
        c["zfr"] = rsend(ref, xf, z, PR + QA, QB, zdev)
        c["fql"].wait_recv()
        c["zfl"] = rsend(ref, xf, z, PR, QA, zdev)

    def row_end(c, names):
        for name in names:
            c[name].wait_recv()

    og = col_own(og_all)
    g_load.wait()
    gc = row_own(g_all)
    u_load.wait()
    uc = row_own(u_all)
    col_mid(og_all, og)
    col_late(og_all, og)
    inp = col_own(in_all)
    col_end(og)
    dw_load.wait()

    @pl.loop(0, FB // 256)
    def _(j):
        cols = pl.ds(pl.multiple_of(j * 256, 256), 256)
        part[:, cols] = nt(og_all[...], dw[cols, :]).astype(BF16)

    def prow(xx, zz, off):
        return (xx * 2 + zz) * 128 + off

    slot = [0]

    def psend(xx, zz, off, n, dev):
        at = slot[0]
        slot[0] += n
        return send(rows(part, prow(xx, zz, off), n), landed.at[pl.ds(at, n), :], dev), at

    def add(xx, zz, off, at, n):
        @pl.loop(0, n // 16)
        def _(i):
            here = pl.ds(pl.multiple_of(prow(xx, zz, off) + i * 16, 16), 16)
            there = pl.ds(pl.multiple_of(at + i * 16, 16), 16)
            part[here, :] = (part[here, :].astype(F32) + landed[there, :].astype(F32)).astype(BF16)

    order = (xf, xl, xr, x)
    zs = [psend(xx, oz, PR, QR, zdev) for xx in order]
    far_r = [psend(xf, zz, 0, PA, rtdev) for zz in (oz, z)]
    far_l = [psend(xf, zz, PA, PB, ldev) for zz in (oz, z)]
    row_mid(g_all, gc)
    for (copy, at), xx in zip(zs, order):
        copy.wait_recv()
        add(xx, z, PR, at, QR)
        if xx is xf:
            far_rq = psend(xf, z, PR + QA, QB, rtdev)
            far_lq = psend(xf, z, PR, QA, ldev)
    for (copy, at), zz in zip(far_r, (oz, z)):
        copy.wait_recv()
        add(xr, zz, 0, at, PA)
    nb_r = [psend(xr, oz, 0, PR, rtdev)]
    for (copy, at), zz in zip(far_l, (oz, z)):
        copy.wait_recv()
        add(xl, zz, PA, at, PB)
    nb_l = [psend(xl, oz, 0, PR, ldev)]
    far_rq[0].wait_recv()
    add(xr, z, PR + QA, far_rq[1], QB)
    nb_r.append(psend(xr, z, 0, 128, rtdev))
    far_lq[0].wait_recv()
    add(xl, z, PR, far_lq[1], QA)
    nb_l.append(psend(xl, z, 0, 128, ldev))

    row_mid(u_all, uc)
    row_late(g_all, gc)
    col_mid(in_all, inp)
    col_late(in_all, inp)

    nb_r[0][0].wait_recv()
    nb_l[0][0].wait_recv()
    add(x, oz, 0, nb_r[0][1], PR)
    add(x, oz, 0, nb_l[0][1], PR)
    last = psend(x, oz, 0, PR, zdev)
    row_late(u_all, uc)
    nb_r[1][0].wait_recv()
    nb_l[1][0].wait_recv()
    last[0].wait_recv()

    def own(lo, hi, landings):
        @pl.loop(lo // 16, hi // 16)
        def _(i):
            here = pl.ds(pl.multiple_of(row * 128 + i * 16, 16), 16)
            total = part[here, :].astype(F32)
            for at in landings:
                total = total + landed[pl.ds(pl.multiple_of(at + i * 16, 16), 16), :].astype(F32)
            h_all[here, :] = total.astype(BF16)

    own(0, PR, (nb_r[1][1], nb_l[1][1], last[1]))
    own(PR, 128, (nb_r[1][1], nb_l[1][1]))

    hc = row_own(h_all)

    col_end(inp)
    outs = [local(in_all, inputs_out), local(og_all, out_grad_out)]
    row_end(gc, ("zq", "zql", "zqr", "fpr", "fpl", "gpr", "gpl", "zfr", "zfl"))
    row_end(uc, ("zq", "zql", "zqr", "fpr", "fpl", "gpr", "gpl", "zfr", "zfl"))

    def pointwise(xx):
        @pl.loop(0, 16)
        def _(i):
            here = pl.ds(pl.multiple_of(xx * 256 + i * 16, 16), 16)
            for j in range(FB // 256):
                cols = pl.ds(j * 256, 256)
                gv = g_all[here, cols].astype(F32)
                uv = u_all[here, cols].astype(F32)
                hv = h_all[here, cols].astype(F32)
                s = jax.nn.sigmoid(gv)
                gs = gv * s
                hid[here, cols] = (gs * uv).astype(BF16)
                gd[here, cols] = (hv * uv * s * (1.0 + gv * (1.0 - s))).astype(BF16)
                ud[here, cols] = (hv * gs).astype(BF16)

    def group(k, xx):
        pointwise(xx)
        for ref, out in ((hid, hidden_out), (gd, gate_out), (ud, up_out)):
            outs.append(local(rows(ref, xx * 256, 256), rows(out, xx * 256, 256)))
        here = pl.ds(pl.multiple_of(xx * 256, 256), 256)

        @pl.loop(0, DB // 256)
        def _(j):
            cols = pl.ds(pl.multiple_of(j * 256, 256), 256)
            act_part[k, :, cols] = (nt(gd[here, :], gw[cols, :]) + nt(ud[here, :], uw[cols, :])).astype(BF16)

        return [
            send(act_part.at[k, pl.ds(pl.multiple_of(j * 128 + ocore * 64, 64), 64), :], sib_in.at[k, j], sdev)
            for j in range(2)
        ]

    def reduce_y(k, xx, sib):
        for j in range(2):
            sib[j].wait_recv()
            mine = act_part[k, pl.ds(pl.multiple_of(j * 128 + core * 64, 64), 64), :]
            y_out[k, j] = (mine.astype(F32) + sib_in[k, j].astype(F32)).astype(BF16)
        copies = []
        for step in (1, 2, 3):
            to = lax.rem(y + 4 - step, 4)
            copy = make(y_out.at[k, lax.rem(to, 2)], y_in.at[k, step - 1], cdev(zh, to, core))
            goes = lax.div(to, 2) == lax.rem(xx, 2)

            @pl.when(goes)
            def _():
                copy.start()

            copies.append((copy, goes))
        return copies

    def reduce_end(k, xx, copies, zcopy):
        @pl.when(lax.div(y, 2) == lax.rem(xx, 2))
        def _():
            for copy, _ in copies:
                copy.wait_recv()
            total = y_out[k, lax.rem(y, 2)].astype(F32)
            for i in range(3):
                total = total + y_in[k, i].astype(F32)

            @pl.when(lax.div(xx, 2) == zh)
            def _():
                final[...] = total

            @pl.when(lax.div(xx, 2) != zh)
            def _():
                z_out[...] = total.astype(BF16)
                zcopy.start()

        for copy, goes in copies:
            @pl.when(goes)
            def _():
                copy.wait_send()

    gw_load.wait()
    uw_load.wait()
    zcopy = make(z_out, z_in, hdev)

    row_mid(h_all, hc)
    hc["zq"].wait_recv()
    s0 = group(0, x)
    row_late(h_all, hc)
    y0 = reduce_y(0, x, s0)
    row_end(hc, ("zql",))
    s1 = group(1, xl)
    reduce_end(0, x, y0, zcopy)
    y1 = reduce_y(1, xl, s1)
    row_end(hc, ("zqr",))
    s2 = group(2, xr)
    reduce_end(1, xl, y1, zcopy)
    y2 = reduce_y(2, xr, s2)
    row_end(hc, ("fpr", "fpl", "gpr", "gpl", "zfr", "zfl"))
    s3 = group(3, xf)
    reduce_end(2, xr, y2, zcopy)
    y3 = reduce_y(3, xf, s3)
    reduce_end(3, xf, y3, zcopy)
    zcopy.wait()
    act_grad[...] = (final[...] + z_in[...].astype(F32)).astype(BF16)
    for copy in outs:
        copy.wait()
    for copy in pending:
        copy.wait_send()
    assert count[0] == N_SEMS, count[0]


def exchange(*args):
    any_spec = pl.BlockSpec(memory_space=pl.ANY)
    vmem = pl.BlockSpec(memory_space=pltpu.VMEM)
    shape = jax.ShapeDtypeStruct
    wide = pltpu.VMEM((T, FB), BF16)
    return pl.pallas_call(
        kernel,
        out_shape=(
            shape((64, DB), BF16),
            shape((T, DB), BF16),
            shape((T, DB), BF16),
            shape((T, FB), BF16),
            shape((T, FB), BF16),
            shape((T, FB), BF16),
        ),
        in_specs=[vmem] * 4 + [any_spec] * 5,
        out_specs=(vmem,) + (any_spec,) * 5,
        scratch_shapes=[
            wide, wide, wide, wide,
            pltpu.VMEM((4 * QR + 2 * PR + QR + 2 * (128 + PR) + PR, FB), BF16),
            pltpu.VMEM((T, DB), BF16),
            pltpu.VMEM((T, DB), BF16),
            pltpu.VMEM((FB, DB), BF16),
            pltpu.VMEM((DB, FB), BF16),
            pltpu.VMEM((DB, FB), BF16),
            wide, wide, wide,
            pltpu.VMEM((4, 256, DB), BF16),
            pltpu.VMEM((4, 2, 64, DB), BF16),
            pltpu.VMEM((4, 2, 64, DB), BF16),
            pltpu.VMEM((4, 3, 64, DB), BF16),
            pltpu.VMEM((64, DB), BF16),
            pltpu.VMEM((64, DB), BF16),
            pltpu.VMEM((64, DB), F32),
            pltpu.SemaphoreType.DMA((N_SEMS,)),
            pltpu.SemaphoreType.DMA((N_SEMS,)),
            pltpu.SemaphoreType.DMA((32,)),
        ],
        compiler_params=pltpu.CompilerParams(
            collective_id=0, has_side_effects=True, vmem_limit_bytes=60 * 2**20
        ),
        name="exchange",
    )(*args)


def contract_first(left, right):
    return lax.dot_general(left, right, (((0,), (0,)), ((), ())), preferred_element_type=F32)


def shards(*args):
    act_grad, inputs, out_grad, hidden, gate, up = exchange(*args)
    factor = 1.0 / math.sqrt(T)
    down_grad = (contract_first(hidden, out_grad) * factor).astype(BF16)
    gate_grad = (contract_first(inputs, gate) * factor).astype(BF16)
    up_grad = (contract_first(inputs, up) * factor).astype(BF16)
    return act_grad, gate_grad, up_grad, down_grad


def solution(mesh):
    rc, cr = P("row", "col"), P("col", "row")
    return jax.shard_map(
        shards,
        mesh=mesh,
        in_specs=(cr, cr, cr, cr, rc, rc, rc, rc, cr),
        out_specs=(cr, rc, rc, cr),
        check_vma=False,
    )
```

```python
import math

import jax
import jax.numpy as jnp
from jax import lax
from jax.experimental import pallas as pl
from jax.experimental.pallas import tpu as pltpu
from jax.sharding import PartitionSpec as P

MESH = pl.DeviceIdType.MESH
T, DB, FB = 1024, 1024, 1792
LIMIT = 46
F32, BF16 = jnp.float32, jnp.bfloat16
FACTOR = 1.0 / math.sqrt(T)
SPLIT_G, SPLIT_H = (80, 48, 32, 16), (80, 48, 48, 32)
SPLIT_U = (64, 64, 32, 32)
PR, QR, PA, QA = 80, 48, 48, 32
PB, QB = PR - PA, QR - QA

N_SEMS = 3 * 16 + 15 + 2 * 17 + 8 * 4 + 1


def nt(a, b):
    return lax.dot_general(a, b, (((1,), (1,)), ((), ())), preferred_element_type=F32)


def tn(a, b):
    return lax.dot_general(a, b, (((0,), (0,)), ((), ())), preferred_element_type=F32)


def rows(ref, start, n):
    return ref.at[pl.ds(pl.multiple_of(start, 16), n), :]


def kernel(
    act_q, act_scale, grad_q, grad_scale, gate_pre, up_pre, gate_w, up_w, down_w,
    act_grad, part, dw, in_t, ud,
    g_all, u_all, h_all, landed, og_all, in_all, gw, uw,
    hid, gd, act_part, sib_in, y_out, y_in, z_out, z_in, final,
    send_sems, recv_sems, local_sems,
):
    row, col = lax.axis_index("row"), lax.axis_index("col")
    x, z = lax.div(row, 2), lax.rem(row, 2)
    zh, y, core = lax.div(col, 8), lax.rem(lax.div(col, 2), 4), lax.rem(col, 2)
    xl, xr, xf = lax.rem(x + 3, 4), lax.rem(x + 1, 4), lax.rem(x + 2, 4)
    yl, yr, yf = lax.rem(y + 3, 4), lax.rem(y + 1, 4), lax.rem(y + 2, 4)
    oz, ozh, ocore = 1 - z, 1 - zh, 1 - core

    def rdev(xx, zz):
        return (xx * 2 + zz, col)

    def cidx(hh, yy, cc):
        return hh * 8 + yy * 2 + cc

    def cdev(hh, yy, cc):
        return (row, cidx(hh, yy, cc))

    zdev, ldev, rtdev = rdev(x, oz), rdev(xl, z), rdev(xr, z)
    hdev, yldev, yrdev, yfdev = cdev(ozh, y, core), cdev(zh, yl, core), cdev(zh, yr, core), cdev(zh, yf, core)
    sdev = cdev(zh, y, ocore)

    count = [0]
    pending = []

    def make(src, dst, dev):
        i = count[0]
        count[0] += 1
        return pltpu.make_async_remote_copy(
            src_ref=src, dst_ref=dst, send_sem=send_sems.at[i], recv_sem=recv_sems.at[i],
            device_id=dev, device_id_type=MESH,
        )

    def send(src, dst, dev):
        copy = make(src, dst, dev)
        copy.start()
        pending.append(copy)
        return copy

    local_count = [0]

    def local(src, dst):
        copy = pltpu.make_async_copy(src, dst, local_sems.at[local_count[0]])
        local_count[0] += 1
        copy.start()
        return copy

    g_load = local(gate_pre, rows(g_all, row * 128, 128))
    u_load = local(up_pre, rows(u_all, row * 128, 128))
    dw_load = local(down_w, dw)
    gw_load = local(gate_w, gw)
    uw_load = local(up_w, uw)

    barrier = pltpu.get_barrier_semaphore()
    partners = (zdev, ldev, rtdev, hdev, yldev, yrdev, yfdev, sdev)
    for dev in partners:
        pl.semaphore_signal(barrier, inc=1, device_id=dev, device_id_type=MESH)

    act_s, grad_s = act_scale[...].T, grad_scale[...].T
    for blk in range(8):
        lanes = pl.ds(blk * 128, 128)
        og_all[pl.ds(pl.multiple_of(col * 64, 64), 64), lanes] = (
            grad_q[:, lanes].astype(F32) * grad_s[:, blk : blk + 1]
        ).astype(BF16)
        in_all[pl.ds(pl.multiple_of(col * 64, 64), 64), lanes] = (
            act_q[:, lanes].astype(F32) * act_s[:, blk : blk + 1]
        ).astype(BF16)

    pl.semaphore_wait(barrier, len(partners))

    def ctile(ref, hh, yy, cc, off=0, n=64):
        return rows(ref, cidx(hh, yy, cc) * 64 + off, n)

    def csend(ref, hh, yy, cc, dev, off=0, n=64):
        where = ctile(ref, hh, yy, cc, off, n)
        return send(where, where, dev)

    def col_own(ref):
        return dict(
            h=csend(ref, zh, y, core, hdev),
            r=csend(ref, zh, y, core, yrdev),
            l=csend(ref, zh, y, core, yldev),
            s=[csend(ref, zh, y, core, sdev)],
        )

    def col_mid(ref, c):
        c["h"].wait_recv()
        c["hr"] = csend(ref, ozh, y, core, yrdev)
        c["hl"] = csend(ref, ozh, y, core, yldev)
        c["s"].append(csend(ref, ozh, y, core, sdev))
        c["r"].wait_recv()
        c["fr"] = csend(ref, zh, yl, core, yrdev, 0, 32)
        c["s"].append(csend(ref, zh, yl, core, sdev))
        c["l"].wait_recv()
        c["fl"] = csend(ref, zh, yr, core, yldev, 32, 32)
        c["s"].append(csend(ref, zh, yr, core, sdev))

    def col_late(ref, c):
        c["hr"].wait_recv()
        c["hfr"] = csend(ref, ozh, yl, core, yrdev, 0, 32)
        c["s"].append(csend(ref, ozh, yl, core, sdev))
        c["hl"].wait_recv()
        c["hfl"] = csend(ref, ozh, yr, core, yldev, 32, 32)
        c["s"].append(csend(ref, ozh, yr, core, sdev))
        c["fr"].wait_recv()
        c["fl"].wait_recv()
        c["s"].append(csend(ref, zh, yf, core, sdev))
        c["hfr"].wait_recv()
        c["hfl"].wait_recv()
        c["s"].append(csend(ref, ozh, yf, core, sdev))

    def col_end(c):
        for copy in c["s"]:
            copy.wait_recv()

    def rsend(ref, xx, zz, off, n, dev):
        where = rows(ref, (xx * 2 + zz) * 128 + off, n)
        return send(where, where, dev)

    def row_own(ref, split):
        PR, QR, _, _ = split
        return dict(
            zp=rsend(ref, x, z, 0, PR, zdev),
            r=rsend(ref, x, z, 0, 128, rtdev),
            l=rsend(ref, x, z, 0, 128, ldev),
            zq=rsend(ref, x, z, PR, QR, zdev),
        )

    def row_mid(ref, c, split):
        PR, QR, PA, QA = split
        PB, QB = PR - PA, QR - QA
        c["zp"].wait_recv()
        c["pr"] = rsend(ref, x, oz, 0, PR, rtdev)
        c["pl"] = rsend(ref, x, oz, 0, PR, ldev)
        c["r"].wait_recv()
        c["fqr"] = rsend(ref, xl, z, PR + QA, QB, rtdev)
        c["zql"] = rsend(ref, xl, z, PR, QR, zdev)
        c["fpr"] = rsend(ref, xl, z, 0, PA, rtdev)
        c["l"].wait_recv()
        c["fql"] = rsend(ref, xr, z, PR, QA, ldev)
        c["zqr"] = rsend(ref, xr, z, PR, QR, zdev)
        c["fpl"] = rsend(ref, xr, z, PA, PB, ldev)

    def row_late(ref, c, split):
        PR, QR, PA, QA = split
        PB, QB = PR - PA, QR - QA
        c["pr"].wait_recv()
        c["gpr"] = rsend(ref, xl, oz, 0, PA, rtdev)
        c["pl"].wait_recv()
        c["gpl"] = rsend(ref, xr, oz, PA, PB, ldev)
        c["fqr"].wait_recv()
        c["zfr"] = rsend(ref, xf, z, PR + QA, QB, zdev)
        c["fql"].wait_recv()
        c["zfl"] = rsend(ref, xf, z, PR, QA, zdev)

    def sent(copies):
        for copy in copies:
            copy.wait_send()
            pending[:] = [other for other in pending if other is not copy]

    def row_end(c, names):
        for name in names:
            c[name].wait_recv()

    og = col_own(og_all)
    g_load.wait()
    gc = row_own(g_all, SPLIT_G)
    u_load.wait()
    uc = row_own(u_all, SPLIT_U)
    col_mid(og_all, og)
    col_late(og_all, og)
    inp = col_own(in_all)
    col_end(og)
    dw_load.wait()

    @pl.loop(0, FB // 256)
    def _(j):
        cols = pl.ds(pl.multiple_of(j * 256, 256), 256)
        part[:, cols] = nt(og_all[...], dw[cols, :]).astype(BF16)

    def prow(xx, zz, off):
        return (xx * 2 + zz) * 128 + off

    slot = [0]

    def psend(xx, zz, off, n, dev):
        at = slot[0]
        slot[0] += n
        return send(rows(part, prow(xx, zz, off), n), landed.at[pl.ds(at, n), :], dev), at

    def add(xx, zz, off, at, n):
        @pl.loop(0, n // 16)
        def _(i):
            here = pl.ds(pl.multiple_of(prow(xx, zz, off) + i * 16, 16), 16)
            there = pl.ds(pl.multiple_of(at + i * 16, 16), 16)
            part[here, :] = (part[here, :].astype(F32) + landed[there, :].astype(F32)).astype(BF16)

    order = (xf, xl, xr, x)
    zs = [psend(xx, oz, PR, QR, zdev) for xx in order]
    far_r = [psend(xf, zz, 0, PA, rtdev) for zz in (oz, z)]
    far_l = [psend(xf, zz, PA, PB, ldev) for zz in (oz, z)]
    row_mid(g_all, gc, SPLIT_G)
    for (copy, at), xx in zip(zs, order):
        copy.wait_recv()
        add(xx, z, PR, at, QR)
        if xx is xf:
            far_rq = psend(xf, z, PR + QA, QB, rtdev)
            far_lq = psend(xf, z, PR, QA, ldev)
    for (copy, at), zz in zip(far_r, (oz, z)):
        copy.wait_recv()
        add(xr, zz, 0, at, PA)
    nb_r = [psend(xr, oz, 0, PR, rtdev)]
    for (copy, at), zz in zip(far_l, (oz, z)):
        copy.wait_recv()
        add(xl, zz, PA, at, PB)
    nb_l = [psend(xl, oz, 0, PR, ldev)]
    far_rq[0].wait_recv()
    add(xr, z, PR + QA, far_rq[1], QB)
    nb_r.append(psend(xr, z, 0, 128, rtdev))
    far_lq[0].wait_recv()
    add(xl, z, PR, far_lq[1], QA)
    nb_l.append(psend(xl, z, 0, 128, ldev))

    row_mid(u_all, uc, SPLIT_U)
    row_late(g_all, gc, SPLIT_G)
    col_mid(in_all, inp)
    col_late(in_all, inp)

    nb_r[0][0].wait_recv()
    nb_l[0][0].wait_recv()
    add(x, oz, 0, nb_r[0][1], PR)
    add(x, oz, 0, nb_l[0][1], PR)
    last = psend(x, oz, 0, PR, zdev)
    row_late(u_all, uc, SPLIT_U)
    nb_r[1][0].wait_recv()
    nb_l[1][0].wait_recv()
    last[0].wait_recv()

    def own(lo, hi, landings):
        @pl.loop(lo // 16, hi // 16)
        def _(i):
            here = pl.ds(pl.multiple_of(row * 128 + i * 16, 16), 16)
            total = part[here, :].astype(F32)
            for at in landings:
                total = total + landed[pl.ds(pl.multiple_of(at + i * 16, 16), 16), :].astype(F32)
            h_all[here, :] = total.astype(BF16)

    own(0, PR, (nb_r[1][1], nb_l[1][1], last[1]))
    own(PR, 128, (nb_r[1][1], nb_l[1][1]))

    hc = row_own(h_all, SPLIT_H)

    col_end(inp)
    row_end(gc, ("zq", "zql", "zqr", "fpr", "fpl", "gpr", "gpl", "zfr", "zfl"))
    row_end(uc, ("zq", "zql", "zqr", "fpr", "fpl", "gpr", "gpl", "zfr", "zfl"))

    @pl.loop(0, T // 16)
    def _(i):
        here = pl.ds(pl.multiple_of(i * 16, 16), 16)
        for j in range(FB // 256):
            cols = pl.ds(j * 256, 256)
            gv = g_all[here, cols].astype(F32)
            hid[here, cols] = (gv * jax.nn.sigmoid(gv) * u_all[here, cols].astype(F32)).astype(BF16)

    @pl.loop(0, FB // 256)
    def _(j):
        cols = pl.ds(pl.multiple_of(j * 256, 256), 256)
        dw[cols, :] = (tn(hid[:, cols], og_all[...]) * FACTOR).astype(BF16)


    places = [(xl, z), (xr, z), (x, z), (x, oz), (xl, oz), (xr, oz), (xf, z), (xf, oz)]
    for pos, (xx, zz) in enumerate(places):
        in_t[:, pos * 128 : pos * 128 + 128] = in_all[pl.ds(pl.multiple_of((xx * 2 + zz) * 128, 128), 128), :].T

    def pointwise(at, to):
        @pl.loop(0, 8)
        def _(i):
            here = pl.ds(pl.multiple_of(at + i * 16, 16), 16)
            there = pl.ds(pl.multiple_of(to + i * 16, 16), 16)
            for j in range(FB // 256):
                cols = pl.ds(j * 256, 256)
                gv = g_all[here, cols].astype(F32)
                hv = h_all[here, cols].astype(F32)
                s = jax.nn.sigmoid(gv)
                gd[there, cols] = (hv * u_all[here, cols].astype(F32) * s * (1.0 + gv * (1.0 - s))).astype(BF16)
                ud[there, cols] = (hv * gv * s).astype(BF16)

    def gate_half(half):
        here = pl.ds(half * 512, 512)
        part[here, :] = (jnp.dot(in_t[here, :], gd[...], preferred_element_type=F32) * FACTOR).astype(BF16)

    def block(pos):
        xx, zz = places[pos]
        at = xx * 2 + zz
        return pos, at, lax.rem(at, 4), lax.div(at, 4)

    def group(blocks):
        here = pl.ds(blocks[0][0] * 128, 128 * len(blocks))
        for pos, at, _, _ in blocks:
            pointwise(at * 128, pos * 128)

        @pl.loop(0, DB // 256)
        def _(j):
            cols = pl.ds(pl.multiple_of(j * 256, 256), 256)
            act_part[here, cols] = (nt(gd[here, :], gw[cols, :]) + nt(ud[here, :], uw[cols, :])).astype(BF16)

        return [send(rows(act_part, pos * 128 + ocore * 64, 64), sib_in.at[pos], sdev) for pos, _, _, _ in blocks]

    def reduce_y(blocks, sib):
        copies = []
        for (i, _, yd, _), copy in zip(blocks, sib):
            copy.wait_recv()
            mine = act_part[pl.ds(pl.multiple_of(i * 128 + core * 64, 64), 64), :]
            y_out[i] = (mine.astype(F32) + sib_in[i].astype(F32)).astype(BF16)
            for step in (1, 2, 3):
                copy = make(y_out.at[i], y_in.at[i, step - 1], cdev(zh, yd, core))
                goes = lax.rem(yd + step, 4) == y

                @pl.when(goes)
                def _():
                    copy.start()

                copies.append((copy, goes))
        return copies

    def reduce_end(blocks, copies, zcopy):
        for b, (i, _, yd, zd) in enumerate(blocks):
            three = copies[3 * b : 3 * b + 3]

            @pl.when(y == yd)
            def _():
                for copy, _ in three:
                    copy.wait_recv()
                total = y_out[i].astype(F32)
                for k in range(3):
                    total = total + y_in[i, k].astype(F32)

                @pl.when(zd == zh)
                def _():
                    final[...] = total

                @pl.when(zd != zh)
                def _():
                    z_out[...] = total.astype(BF16)
                    zcopy.start()

            for copy, goes in three:
                @pl.when(goes)
                def _():
                    copy.wait_send()

    gw_load.wait()
    uw_load.wait()
    zcopy = make(z_out, z_in, hdev)

    row_mid(h_all, hc, SPLIT_H)
    work = [[block(0), block(1)], [block(2), block(3)], [block(4), block(5)], [block(6)], [block(7)]]
    s0 = group(work[0])
    row_end(hc, ("zq",))
    s1 = group(work[1])
    row_late(h_all, hc, SPLIT_H)
    y0 = reduce_y(work[0], s0)
    y1 = reduce_y(work[1], s1)
    row_end(hc, ("zql", "zqr"))
    s2 = group(work[2])
    reduce_end(work[0], y0, zcopy)
    reduce_end(work[1], y1, zcopy)
    row_end(hc, ("fpr", "fpl"))
    s3 = group(work[3])
    y2 = reduce_y(work[2], s2)
    row_end(hc, ("gpr", "gpl", "zfr", "zfl"))
    s4 = group(work[4])
    y3 = reduce_y(work[3], s3)
    reduce_end(work[2], y2, zcopy)
    sent([copy for copy, _ in zs + far_r + far_l + nb_r + nb_l + [far_rq, far_lq, last]])
    y4 = reduce_y(work[4], s4)
    gate_half(0)
    reduce_end(work[3], y3, zcopy)
    gate_half(1)
    reduce_end(work[4], y4, zcopy)
    zcopy.wait()
    act_grad[...] = (final[...] + z_in[...].astype(F32)).astype(BF16)
    for copy in pending:
        copy.wait_send()
    assert count[0] == N_SEMS, count[0]


def exchange(*args):
    any_spec = pl.BlockSpec(memory_space=pl.ANY)
    vmem = pl.BlockSpec(memory_space=pltpu.VMEM)
    wide = pltpu.VMEM((T, FB), BF16)
    return pl.pallas_call(
        kernel,
        out_shape=(
            pltpu.VMEM((64, DB), BF16),
            pltpu.VMEM((DB, FB), BF16),
            pltpu.VMEM((FB, DB), BF16),
            pltpu.VMEM((DB, T), BF16),
            pltpu.VMEM((T, FB), BF16),
        ),
        in_specs=[vmem] * 4 + [any_spec] * 5,
        out_specs=(vmem,) * 5,
        scratch_shapes=[
            wide, wide, wide,
            pltpu.VMEM((4 * QR + 2 * PR + QR + 2 * (128 + PR) + PR, FB), BF16),
            pltpu.VMEM((T, DB), BF16),
            pltpu.VMEM((T, DB), BF16),
            pltpu.VMEM((DB, FB), BF16),
            pltpu.VMEM((DB, FB), BF16),
            wide, wide,
            pltpu.VMEM((T, DB), BF16),
            pltpu.VMEM((8, 64, DB), BF16),
            pltpu.VMEM((8, 64, DB), BF16),
            pltpu.VMEM((8, 3, 64, DB), BF16),
            pltpu.VMEM((64, DB), BF16),
            pltpu.VMEM((64, DB), BF16),
            pltpu.VMEM((64, DB), F32),
            pltpu.SemaphoreType.DMA((N_SEMS,)),
            pltpu.SemaphoreType.DMA((N_SEMS,)),
            pltpu.SemaphoreType.DMA((32,)),
        ],
        compiler_params=pltpu.CompilerParams(
            collective_id=0, has_side_effects=True, vmem_limit_bytes=LIMIT * 2**20
        ),
        name="exchange",
    )(*args)


STEPS = FB // 256


def finish_kernel(in_t, delta, act, gate, down, up_grad, act_grad, gate_grad, down_grad, up, sems):
    copies = [
        pltpu.make_async_copy(act, act_grad, sems.at[0]),
        pltpu.make_async_copy(down, down_grad, sems.at[1]),
        pltpu.make_async_copy(gate, gate_grad, sems.at[2]),
    ]
    for copy in copies:
        copy.start()
    for half in range(2):
        here = pl.ds(half * 512, 512)
        up[here, :] = (jnp.dot(in_t[here, :], delta[...], preferred_element_type=F32) * FACTOR).astype(BF16)
        copies.append(pltpu.make_async_copy(up.at[here, :], up_grad.at[here, :], sems.at[3 + half]))
        copies[-1].start()
    for copy in copies:
        copy.wait()


def finish(in_t, delta, act, gate, down):
    any_spec = pl.BlockSpec(memory_space=pl.ANY)
    vmem = pl.BlockSpec(memory_space=pltpu.VMEM)
    up, act, gate, down = pl.pallas_call(
        finish_kernel,
        out_shape=(
            jax.ShapeDtypeStruct((DB, FB), BF16),
            jax.ShapeDtypeStruct(act.shape, BF16),
            jax.ShapeDtypeStruct(gate.shape, BF16),
            jax.ShapeDtypeStruct(down.shape, BF16),
        ),
        in_specs=[vmem] * 5,
        out_specs=(any_spec,) * 4,
        scratch_shapes=[pltpu.VMEM((DB, FB), BF16), pltpu.SemaphoreType.DMA((5,))],
        compiler_params=pltpu.CompilerParams(vmem_limit_bytes=24 * 2**20),
        name="finish",
    )(in_t, delta, act, gate, down)
    return act, gate, up, down


def shards(act_q, act_scale, grad_q, grad_scale, *args):
    act, gate, down, in_t, delta = exchange(act_q, act_scale.T, grad_q, grad_scale.T, *args)
    return finish(in_t, delta, act, gate, down)


def solution(mesh):
    rc, cr = P("row", "col"), P("col", "row")
    return jax.shard_map(
        shards,
        mesh=mesh,
        in_specs=(cr, cr, cr, cr, rc, rc, rc, rc, cr),
        out_specs=(cr, rc, rc, cr),
        check_vma=False,
    )
```

```python
import math

import jax
import jax.numpy as jnp
from jax import lax
from jax.experimental import pallas as pl
from jax.experimental.pallas import tpu as pltpu
from jax.sharding import PartitionSpec as P

MESH = pl.DeviceIdType.MESH
T, DB, FB = 1024, 1024, 1792
LIMIT = 46
F32, BF16 = jnp.float32, jnp.bfloat16
FACTOR = 1.0 / math.sqrt(T)
SPLIT_G, SPLIT_H = (80, 48, 32, 16), (80, 48, 48, 32)
SPLIT_U = (64, 64, 32, 32)
PR, QR, PA, QA = 80, 48, 48, 32
PB, QB = PR - PA, QR - QA

N_SEMS = 3 * 16 + 15 + 2 * 17 + 8 * 7 + 1


def nt(a, b):
    return lax.dot_general(a, b, (((1,), (1,)), ((), ())), preferred_element_type=F32)


def tn(a, b):
    return lax.dot_general(a, b, (((0,), (0,)), ((), ())), preferred_element_type=F32)


def rows(ref, start, n):
    return ref.at[pl.ds(pl.multiple_of(start, 16), n), :]


def kernel(
    act_q, act_scale, grad_q, grad_scale, gate_pre, up_pre, gate_w, up_w, down_w,
    act_grad, part, dw, g_all,
    u_all, h_all, landed, og_all, in_all, gw, uw,
    hid, gd, ud, in_t, act_part, sib_in, y_out, y_far, y_in, z_out, z_in, final,
    send_sems, recv_sems, local_sems,
):
    row, col = lax.axis_index("row"), lax.axis_index("col")
    x, z = lax.div(row, 2), lax.rem(row, 2)
    zh, y, core = lax.div(col, 8), lax.rem(lax.div(col, 2), 4), lax.rem(col, 2)
    xl, xr, xf = lax.rem(x + 3, 4), lax.rem(x + 1, 4), lax.rem(x + 2, 4)
    yl, yr, yf = lax.rem(y + 3, 4), lax.rem(y + 1, 4), lax.rem(y + 2, 4)
    oz, ozh, ocore = 1 - z, 1 - zh, 1 - core

    def rdev(xx, zz):
        return (xx * 2 + zz, col)

    def cidx(hh, yy, cc):
        return hh * 8 + yy * 2 + cc

    def cdev(hh, yy, cc):
        return (row, cidx(hh, yy, cc))

    zdev, ldev, rtdev = rdev(x, oz), rdev(xl, z), rdev(xr, z)
    hdev, yldev, yrdev = cdev(ozh, y, core), cdev(zh, yl, core), cdev(zh, yr, core)
    sdev = cdev(zh, y, ocore)

    count = [0]
    pending = []

    def make(src, dst, dev):
        i = count[0]
        count[0] += 1
        return pltpu.make_async_remote_copy(
            src_ref=src, dst_ref=dst, send_sem=send_sems.at[i], recv_sem=recv_sems.at[i],
            device_id=dev, device_id_type=MESH,
        )

    def send(src, dst, dev):
        copy = make(src, dst, dev)
        copy.start()
        pending.append(copy)
        return copy

    local_count = [0]

    def local(src, dst):
        copy = pltpu.make_async_copy(src, dst, local_sems.at[local_count[0]])
        local_count[0] += 1
        copy.start()
        return copy

    g_load = local(gate_pre, rows(g_all, row * 128, 128))
    u_load = local(up_pre, rows(u_all, row * 128, 128))
    dw_load = local(down_w, dw)
    gw_load = local(gate_w, gw)
    uw_load = local(up_w, uw)

    barrier = pltpu.get_barrier_semaphore()
    partners = (zdev, ldev, rtdev, hdev, yldev, yrdev, sdev)
    for dev in partners:
        pl.semaphore_signal(barrier, inc=1, device_id=dev, device_id_type=MESH)

    act_s, grad_s = act_scale[...].T, grad_scale[...].T
    for blk in range(8):
        lanes = pl.ds(blk * 128, 128)
        og_all[pl.ds(pl.multiple_of(col * 64, 64), 64), lanes] = (
            grad_q[:, lanes].astype(F32) * grad_s[:, blk : blk + 1]
        ).astype(BF16)
        in_all[pl.ds(pl.multiple_of(col * 64, 64), 64), lanes] = (
            act_q[:, lanes].astype(F32) * act_s[:, blk : blk + 1]
        ).astype(BF16)

    pl.semaphore_wait(barrier, len(partners))

    def ctile(ref, hh, yy, cc, off=0, n=64):
        return rows(ref, cidx(hh, yy, cc) * 64 + off, n)

    def csend(ref, hh, yy, cc, dev, off=0, n=64):
        where = ctile(ref, hh, yy, cc, off, n)
        return send(where, where, dev)

    def col_own(ref):
        return dict(
            h=csend(ref, zh, y, core, hdev),
            r=csend(ref, zh, y, core, yrdev),
            l=csend(ref, zh, y, core, yldev),
            s=[csend(ref, zh, y, core, sdev)],
        )

    def col_mid(ref, c):
        c["h"].wait_recv()
        c["hr"] = csend(ref, ozh, y, core, yrdev)
        c["hl"] = csend(ref, ozh, y, core, yldev)
        c["s"].append(csend(ref, ozh, y, core, sdev))
        c["r"].wait_recv()
        c["fr"] = csend(ref, zh, yl, core, yrdev, 0, 32)
        c["s"].append(csend(ref, zh, yl, core, sdev))
        c["l"].wait_recv()
        c["fl"] = csend(ref, zh, yr, core, yldev, 32, 32)
        c["s"].append(csend(ref, zh, yr, core, sdev))

    def col_late(ref, c):
        c["hr"].wait_recv()
        c["hfr"] = csend(ref, ozh, yl, core, yrdev, 0, 32)
        c["s"].append(csend(ref, ozh, yl, core, sdev))
        c["hl"].wait_recv()
        c["hfl"] = csend(ref, ozh, yr, core, yldev, 32, 32)
        c["s"].append(csend(ref, ozh, yr, core, sdev))
        c["fr"].wait_recv()
        c["fl"].wait_recv()
        c["s"].append(csend(ref, zh, yf, core, sdev))
        c["hfr"].wait_recv()
        c["hfl"].wait_recv()
        c["s"].append(csend(ref, ozh, yf, core, sdev))

    def col_end(c):
        for copy in c["s"]:
            copy.wait_recv()

    def rsend(ref, xx, zz, off, n, dev):
        where = rows(ref, (xx * 2 + zz) * 128 + off, n)
        return send(where, where, dev)

    def row_own(ref, split):
        PR, QR, _, _ = split
        return dict(
            zp=rsend(ref, x, z, 0, PR, zdev),
            r=rsend(ref, x, z, 0, 128, rtdev),
            l=rsend(ref, x, z, 0, 128, ldev),
            zq=rsend(ref, x, z, PR, QR, zdev),
        )

    def row_mid(ref, c, split):
        PR, QR, PA, QA = split
        PB, QB = PR - PA, QR - QA
        c["zp"].wait_recv()
        c["pr"] = rsend(ref, x, oz, 0, PR, rtdev)
        c["pl"] = rsend(ref, x, oz, 0, PR, ldev)
        c["r"].wait_recv()
        c["fqr"] = rsend(ref, xl, z, PR + QA, QB, rtdev)
        c["zql"] = rsend(ref, xl, z, PR, QR, zdev)
        c["fpr"] = rsend(ref, xl, z, 0, PA, rtdev)
        c["l"].wait_recv()
        c["fql"] = rsend(ref, xr, z, PR, QA, ldev)
        c["zqr"] = rsend(ref, xr, z, PR, QR, zdev)
        c["fpl"] = rsend(ref, xr, z, PA, PB, ldev)

    def row_late(ref, c, split):
        PR, QR, PA, QA = split
        PB, QB = PR - PA, QR - QA
        c["pr"].wait_recv()
        c["gpr"] = rsend(ref, xl, oz, 0, PA, rtdev)
        c["pl"].wait_recv()
        c["gpl"] = rsend(ref, xr, oz, PA, PB, ldev)
        c["fqr"].wait_recv()
        c["zfr"] = rsend(ref, xf, z, PR + QA, QB, zdev)
        c["fql"].wait_recv()
        c["zfl"] = rsend(ref, xf, z, PR, QA, zdev)

    def sent(copies):
        for copy in copies:
            copy.wait_send()
            pending[:] = [other for other in pending if other is not copy]

    def row_end(c, names):
        for name in names:
            c[name].wait_recv()

    og = col_own(og_all)
    g_load.wait()
    gc = row_own(g_all, SPLIT_G)
    u_load.wait()
    uc = row_own(u_all, SPLIT_U)
    col_mid(og_all, og)
    col_late(og_all, og)
    inp = col_own(in_all)
    col_end(og)
    dw_load.wait()

    @pl.loop(0, FB // 256)
    def _(j):
        cols = pl.ds(pl.multiple_of(j * 256, 256), 256)
        part[:, cols] = nt(og_all[...], dw[cols, :]).astype(BF16)

    def prow(xx, zz, off):
        return (xx * 2 + zz) * 128 + off

    slot = [0]

    def psend(xx, zz, off, n, dev):
        at = slot[0]
        slot[0] += n
        return send(rows(part, prow(xx, zz, off), n), landed.at[pl.ds(at, n), :], dev), at

    def add(xx, zz, off, at, n):
        @pl.loop(0, n // 16)
        def _(i):
            here = pl.ds(pl.multiple_of(prow(xx, zz, off) + i * 16, 16), 16)
            there = pl.ds(pl.multiple_of(at + i * 16, 16), 16)
            part[here, :] = (part[here, :].astype(F32) + landed[there, :].astype(F32)).astype(BF16)

    order = (xf, xl, xr, x)
    zs = [psend(xx, oz, PR, QR, zdev) for xx in order]
    far_r = [psend(xf, zz, 0, PA, rtdev) for zz in (oz, z)]
    far_l = [psend(xf, zz, PA, PB, ldev) for zz in (oz, z)]
    row_mid(g_all, gc, SPLIT_G)
    for (copy, at), xx in zip(zs, order):
        copy.wait_recv()
        add(xx, z, PR, at, QR)
        if xx is xf:
            far_rq = psend(xf, z, PR + QA, QB, rtdev)
            far_lq = psend(xf, z, PR, QA, ldev)
    for (copy, at), zz in zip(far_r, (oz, z)):
        copy.wait_recv()
        add(xr, zz, 0, at, PA)
    nb_r = [psend(xr, oz, 0, PR, rtdev)]
    for (copy, at), zz in zip(far_l, (oz, z)):
        copy.wait_recv()
        add(xl, zz, PA, at, PB)
    nb_l = [psend(xl, oz, 0, PR, ldev)]
    far_rq[0].wait_recv()
    add(xr, z, PR + QA, far_rq[1], QB)
    nb_r.append(psend(xr, z, 0, 128, rtdev))
    far_lq[0].wait_recv()
    add(xl, z, PR, far_lq[1], QA)
    nb_l.append(psend(xl, z, 0, 128, ldev))

    row_mid(u_all, uc, SPLIT_U)
    row_late(g_all, gc, SPLIT_G)
    col_mid(in_all, inp)
    col_late(in_all, inp)

    nb_r[0][0].wait_recv()
    nb_l[0][0].wait_recv()
    add(x, oz, 0, nb_r[0][1], PR)
    add(x, oz, 0, nb_l[0][1], PR)
    last = psend(x, oz, 0, PR, zdev)
    row_late(u_all, uc, SPLIT_U)
    nb_r[1][0].wait_recv()
    nb_l[1][0].wait_recv()
    last[0].wait_recv()

    def own(lo, hi, landings):
        @pl.loop(lo // 16, hi // 16)
        def _(i):
            here = pl.ds(pl.multiple_of(row * 128 + i * 16, 16), 16)
            total = part[here, :].astype(F32)
            for at in landings:
                total = total + landed[pl.ds(pl.multiple_of(at + i * 16, 16), 16), :].astype(F32)
            h_all[here, :] = total.astype(BF16)

    own(0, PR, (nb_r[1][1], nb_l[1][1], last[1]))
    own(PR, 128, (nb_r[1][1], nb_l[1][1]))

    hc = row_own(h_all, SPLIT_H)

    col_end(inp)
    row_end(gc, ("zq", "zql", "zqr", "fpr", "fpl", "gpr", "gpl", "zfr", "zfl"))
    row_end(uc, ("zq", "zql", "zqr", "fpr", "fpl", "gpr", "gpl", "zfr", "zfl"))

    @pl.loop(0, T // 16)
    def _(i):
        here = pl.ds(pl.multiple_of(i * 16, 16), 16)
        for j in range(FB // 256):
            cols = pl.ds(j * 256, 256)
            gv = g_all[here, cols].astype(F32)
            hid[here, cols] = (gv * jax.nn.sigmoid(gv) * u_all[here, cols].astype(F32)).astype(BF16)

    @pl.loop(0, FB // 256)
    def _(j):
        cols = pl.ds(pl.multiple_of(j * 256, 256), 256)
        dw[cols, :] = (tn(hid[:, cols], og_all[...]) * FACTOR).astype(BF16)


    places = [(xl, z), (xr, z), (x, z), (x, oz), (xl, oz), (xr, oz), (xf, z), (xf, oz)]
    for pos, (xx, zz) in enumerate(places):
        in_t[:, pos * 128 : pos * 128 + 128] = in_all[pl.ds(pl.multiple_of((xx * 2 + zz) * 128, 128), 128), :].T

    def pointwise(at, to):
        @pl.loop(0, 8)
        def _(i):
            here = pl.ds(pl.multiple_of(at + i * 16, 16), 16)
            there = pl.ds(pl.multiple_of(to + i * 16, 16), 16)
            for j in range(FB // 256):
                cols = pl.ds(j * 256, 256)
                gv = g_all[here, cols].astype(F32)
                hv = h_all[here, cols].astype(F32)
                s = jax.nn.sigmoid(gv)
                gd[there, cols] = (hv * u_all[here, cols].astype(F32) * s * (1.0 + gv * (1.0 - s))).astype(BF16)
                ud[there, cols] = (hv * gv * s).astype(BF16)

    def weight_grad(delta, total, quarter):
        here = pl.ds(quarter * 256, 256)
        total[here, :] = (jnp.dot(in_t[here, :], delta[...], preferred_element_type=F32) * FACTOR).astype(BF16)

    def block(pos):
        xx, zz = places[pos]
        at = xx * 2 + zz
        return pos, at, lax.rem(at, 4), lax.div(at, 4)

    def group(blocks):
        here = pl.ds(blocks[0][0] * 128, 128 * len(blocks))
        for pos, at, _, _ in blocks:
            pointwise(at * 128, pos * 128)

        @pl.loop(0, DB // 256)
        def _(j):
            cols = pl.ds(pl.multiple_of(j * 256, 256), 256)
            act_part[here, cols] = (nt(gd[here, :], gw[cols, :]) + nt(ud[here, :], uw[cols, :])).astype(BF16)

        return [send(rows(act_part, pos * 128 + ocore * 64, 64), sib_in.at[pos], sdev) for pos, _, _, _ in blocks]

    LO, HI = pl.ds(0, 32), pl.ds(32, 32)

    def reduce_y(blocks, sib):
        result = []
        for (i, _, yd, _), copy in zip(blocks, sib):
            copy.wait_recv()
            mine = act_part[pl.ds(pl.multiple_of(i * 128 + core * 64, 64), 64), :]
            y_out[i] = (mine.astype(F32) + sib_in[i].astype(F32)).astype(BF16)
            where = lax.rem(y + 4 - yd, 4)

            def half(src, dst, dev):
                return make(y_out.at[i, src, :], dst.at[src, :], dev)

            c = dict(
                where=where,
                far_lo=half(LO, y_far.at[i], yldev),
                far_hi=half(HI, y_far.at[i], yrdev),
                l_hi=half(HI, y_in.at[i, 0], yldev),
                l_lo=half(LO, y_in.at[i, 0], yldev),
                r_lo=half(LO, y_in.at[i, 1], yrdev),
                r_hi=half(HI, y_in.at[i, 1], yrdev),
            )

            @pl.when(where == 2)
            def _():
                c["far_lo"].start()
                c["far_hi"].start()

            @pl.when(where == 1)
            def _():
                c["l_hi"].start()

            @pl.when(where == 3)
            def _():
                c["r_lo"].start()

            result.append(c)
        return result

    def relay(blocks, copies):
        for (i, _, _, _), c in zip(blocks, copies):
            for at, part_of, far, on in ((1, LO, "far_lo", "l_lo"), (3, HI, "far_hi", "r_hi")):

                @pl.when(c["where"] == at)
                def _():
                    c[far].wait_recv()
                    y_out[i, part_of, :] = (
                        y_out[i, part_of, :].astype(F32) + y_far[i, part_of, :].astype(F32)
                    ).astype(BF16)
                    c[on].start()

    def reduce_end(blocks, copies, zcopy):
        for (i, _, _, zd), c in zip(blocks, copies):

            @pl.when(c["where"] == 0)
            def _():
                for name in ("l_hi", "r_lo", "l_lo", "r_hi"):
                    c[name].wait_recv()
                total = y_out[i].astype(F32) + y_in[i, 0].astype(F32) + y_in[i, 1].astype(F32)

                @pl.when(zd == zh)
                def _():
                    final[...] = total

                @pl.when(zd != zh)
                def _():
                    z_out[...] = total.astype(BF16)
                    zcopy.start()

            for at, names in ((2, ("far_lo", "far_hi")), (1, ("l_hi", "l_lo")), (3, ("r_lo", "r_hi"))):

                @pl.when(c["where"] == at)
                def _():
                    for name in names:
                        c[name].wait_send()

    gw_load.wait()
    uw_load.wait()
    zcopy = make(z_out, z_in, hdev)

    row_mid(h_all, hc, SPLIT_H)
    work = [[block(0), block(1)], [block(2), block(3)], [block(4), block(5)], [block(6)], [block(7)]]
    s0 = group(work[0])
    row_end(hc, ("zq",))
    s1 = group(work[1])
    row_late(h_all, hc, SPLIT_H)
    y0 = reduce_y(work[0], s0)
    y1 = reduce_y(work[1], s1)
    row_end(hc, ("zql", "zqr"))
    s2 = group(work[2])
    relay(work[0], y0)
    relay(work[1], y1)
    row_end(hc, ("fpr", "fpl"))
    s3 = group(work[3])
    y2 = reduce_y(work[2], s2)
    reduce_end(work[0], y0, zcopy)
    reduce_end(work[1], y1, zcopy)
    row_end(hc, ("gpr", "gpl", "zfr", "zfl"))
    s4 = group(work[4])
    y3 = reduce_y(work[3], s3)
    relay(work[2], y2)
    sent([copy for copy, _ in zs + far_r + far_l + nb_r + nb_l + [far_rq, far_lq, last]])
    y4 = reduce_y(work[4], s4)
    weight_grad(gd, part, 0)
    relay(work[3], y3)
    weight_grad(gd, part, 1)
    relay(work[4], y4)
    reduce_end(work[2], y2, zcopy)
    weight_grad(gd, part, 2)
    reduce_end(work[3], y3, zcopy)
    weight_grad(gd, part, 3)
    reduce_end(work[4], y4, zcopy)
    sent(list(gc.values()))
    for quarter in range(4):
        weight_grad(ud, g_all, quarter)
    zcopy.wait()
    act_grad[...] = (final[...] + z_in[...].astype(F32)).astype(BF16)
    for copy in pending:
        copy.wait_send()
    assert count[0] == N_SEMS, count[0]


def exchange(*args):
    any_spec = pl.BlockSpec(memory_space=pl.ANY)
    vmem = pl.BlockSpec(memory_space=pltpu.VMEM)
    wide = pltpu.VMEM((T, FB), BF16)
    return pl.pallas_call(
        kernel,
        out_shape=(
            pltpu.VMEM((64, DB), BF16),
            pltpu.VMEM((DB, FB), BF16),
            pltpu.VMEM((FB, DB), BF16),
            pltpu.VMEM((DB, FB), BF16),
        ),
        in_specs=[vmem] * 4 + [any_spec] * 5,
        out_specs=(vmem,) * 4,
        scratch_shapes=[
            wide, wide,
            pltpu.VMEM((4 * QR + 2 * PR + QR + 2 * (128 + PR) + PR, FB), BF16),
            pltpu.VMEM((T, DB), BF16),
            pltpu.VMEM((T, DB), BF16),
            pltpu.VMEM((DB, FB), BF16),
            pltpu.VMEM((DB, FB), BF16),
            wide, wide, wide,
            pltpu.VMEM((DB, T), BF16),
            pltpu.VMEM((T, DB), BF16),
            pltpu.VMEM((8, 64, DB), BF16),
            pltpu.VMEM((8, 64, DB), BF16),
            pltpu.VMEM((8, 64, DB), BF16),
            pltpu.VMEM((8, 2, 64, DB), BF16),
            pltpu.VMEM((64, DB), BF16),
            pltpu.VMEM((64, DB), BF16),
            pltpu.VMEM((64, DB), F32),
            pltpu.SemaphoreType.DMA((N_SEMS,)),
            pltpu.SemaphoreType.DMA((N_SEMS,)),
            pltpu.SemaphoreType.DMA((32,)),
        ],
        compiler_params=pltpu.CompilerParams(
            collective_id=0, has_side_effects=True, vmem_limit_bytes=LIMIT * 2**20
        ),
        name="exchange",
    )(*args)


def finish_kernel(*refs):
    copies = [pltpu.make_async_copy(refs[i], refs[4 + i], refs[8].at[i]) for i in range(4)]
    for copy in copies:
        copy.start()
    for copy in copies:
        copy.wait()


def finish(*arrays):
    return pl.pallas_call(
        finish_kernel,
        out_shape=tuple(jax.ShapeDtypeStruct(a.shape, BF16) for a in arrays),
        in_specs=[pl.BlockSpec(memory_space=pltpu.VMEM)] * 4,
        out_specs=(pl.BlockSpec(memory_space=pl.ANY),) * 4,
        scratch_shapes=[pltpu.SemaphoreType.DMA((4,))],
        compiler_params=pltpu.CompilerParams(vmem_limit_bytes=24 * 2**20),
        name="finish",
    )(*arrays)


def shards(act_q, act_scale, grad_q, grad_scale, *args):
    act, gate, down, up = exchange(act_q, act_scale.T, grad_q, grad_scale.T, *args)
    return finish(act, gate, up, down)


def solution(mesh):
    rc, cr = P("row", "col"), P("col", "row")
    return jax.shard_map(
        shards,
        mesh=mesh,
        in_specs=(cr, cr, cr, cr, rc, rc, rc, rc, cr),
        out_specs=(cr, rc, rc, cr),
        check_vma=False,
    )
```

```python
import math

import jax
import jax.numpy as jnp
from jax import lax
from jax.experimental import pallas as pl
from jax.experimental.pallas import tpu as pltpu
from jax.sharding import PartitionSpec as P

MESH = pl.DeviceIdType.MESH
T, DB, FB = 1024, 1024, 1792
LIMIT = 46
F32, BF16 = jnp.float32, jnp.bfloat16
FACTOR = 1.0 / math.sqrt(T)
SPLIT_G, SPLIT_H = (80, 48, 32, 16), (80, 48, 48, 32)
SPLIT_U = (64, 64, 32, 32)
PR, QR, PA, QA = 80, 48, 48, 32
PB, QB = PR - PA, QR - QA

N_SEMS = 3 * 16 + 15 + 2 * 17 + 8 * 7 + 1


def nt(a, b):
    return lax.dot_general(a, b, (((1,), (1,)), ((), ())), preferred_element_type=F32)


def tn(a, b):
    return lax.dot_general(a, b, (((0,), (0,)), ((), ())), preferred_element_type=F32)


def rows(ref, start, n):
    return ref.at[pl.ds(pl.multiple_of(start, 16), n), :]


def kernel(
    act_q, act_scale, grad_q, grad_scale, gate_pre, up_pre, gate_w, up_w, down_w,
    act_grad, part, dw, g_all,
    u_all, h_all, landed, og_all, in_all, gw, uw,
    hid, gd, ud, in_t, act_part, sib_in, y_out, y_far, y_in, z_out, z_in, final,
    send_sems, recv_sems, local_sems,
):
    row, col = lax.axis_index("row"), lax.axis_index("col")
    x, z = lax.div(row, 2), lax.rem(row, 2)
    zh, y, core = lax.div(col, 8), lax.rem(lax.div(col, 2), 4), lax.rem(col, 2)
    xl, xr, xf = lax.rem(x + 3, 4), lax.rem(x + 1, 4), lax.rem(x + 2, 4)
    yl, yr, yf = lax.rem(y + 3, 4), lax.rem(y + 1, 4), lax.rem(y + 2, 4)
    oz, ozh, ocore = 1 - z, 1 - zh, 1 - core

    def rdev(xx, zz):
        return (xx * 2 + zz, col)

    def cidx(hh, yy, cc):
        return hh * 8 + yy * 2 + cc

    def cdev(hh, yy, cc):
        return (row, cidx(hh, yy, cc))

    zdev, ldev, rtdev = rdev(x, oz), rdev(xl, z), rdev(xr, z)
    hdev, yldev, yrdev = cdev(ozh, y, core), cdev(zh, yl, core), cdev(zh, yr, core)
    sdev = cdev(zh, y, ocore)

    count = [0]
    pending = []

    def make(src, dst, dev):
        i = count[0]
        count[0] += 1
        return pltpu.make_async_remote_copy(
            src_ref=src, dst_ref=dst, send_sem=send_sems.at[i], recv_sem=recv_sems.at[i],
            device_id=dev, device_id_type=MESH,
        )

    def send(src, dst, dev):
        copy = make(src, dst, dev)
        copy.start()
        pending.append(copy)
        return copy

    local_count = [0]

    def local(src, dst):
        copy = pltpu.make_async_copy(src, dst, local_sems.at[local_count[0]])
        local_count[0] += 1
        copy.start()
        return copy

    g_load = local(gate_pre, rows(g_all, row * 128, 128))
    u_load = local(up_pre, rows(u_all, row * 128, 128))
    dw_load = local(down_w, dw)
    gw_load = local(gate_w, gw)
    uw_load = local(up_w, uw)

    barrier = pltpu.get_barrier_semaphore()
    partners = (zdev, ldev, rtdev, hdev, yldev, yrdev, sdev)
    for dev in partners:
        pl.semaphore_signal(barrier, inc=1, device_id=dev, device_id_type=MESH)

    def dequantize(values, scales, out):
        by_token = scales[...].T
        for blk in range(8):
            lanes = pl.ds(blk * 128, 128)
            out[pl.ds(pl.multiple_of(col * 64, 64), 64), lanes] = (
                values[:, lanes].astype(F32) * by_token[:, blk : blk + 1]
            ).astype(BF16)

    dequantize(grad_q, grad_scale, og_all)

    pl.semaphore_wait(barrier, len(partners))

    def ctile(ref, hh, yy, cc, off=0, n=64):
        return rows(ref, cidx(hh, yy, cc) * 64 + off, n)

    def csend(ref, hh, yy, cc, dev, off=0, n=64):
        where = ctile(ref, hh, yy, cc, off, n)
        return send(where, where, dev)

    def col_own(ref):
        return dict(
            h=csend(ref, zh, y, core, hdev),
            r=csend(ref, zh, y, core, yrdev),
            l=csend(ref, zh, y, core, yldev),
            s=[csend(ref, zh, y, core, sdev)],
        )

    def col_mid(ref, c):
        c["h"].wait_recv()
        c["hr"] = csend(ref, ozh, y, core, yrdev)
        c["hl"] = csend(ref, ozh, y, core, yldev)
        c["s"].append(csend(ref, ozh, y, core, sdev))
        c["r"].wait_recv()
        c["fr"] = csend(ref, zh, yl, core, yrdev, 0, 32)
        c["s"].append(csend(ref, zh, yl, core, sdev))
        c["l"].wait_recv()
        c["fl"] = csend(ref, zh, yr, core, yldev, 32, 32)
        c["s"].append(csend(ref, zh, yr, core, sdev))

    def col_late(ref, c):
        c["hr"].wait_recv()
        c["hfr"] = csend(ref, ozh, yl, core, yrdev, 0, 32)
        c["s"].append(csend(ref, ozh, yl, core, sdev))
        c["hl"].wait_recv()
        c["hfl"] = csend(ref, ozh, yr, core, yldev, 32, 32)
        c["s"].append(csend(ref, ozh, yr, core, sdev))
        c["fr"].wait_recv()
        c["fl"].wait_recv()
        c["s"].append(csend(ref, zh, yf, core, sdev))
        c["hfr"].wait_recv()
        c["hfl"].wait_recv()
        c["s"].append(csend(ref, ozh, yf, core, sdev))

    def col_end(c):
        for copy in c["s"]:
            copy.wait_recv()

    def rsend(ref, xx, zz, off, n, dev):
        where = rows(ref, (xx * 2 + zz) * 128 + off, n)
        return send(where, where, dev)

    def row_own(ref, split):
        PR, QR, _, _ = split
        return dict(
            zp=rsend(ref, x, z, 0, PR, zdev),
            r=rsend(ref, x, z, 0, 128, rtdev),
            l=rsend(ref, x, z, 0, 128, ldev),
            zq=rsend(ref, x, z, PR, QR, zdev),
        )

    def row_mid(ref, c, split):
        PR, QR, PA, QA = split
        PB, QB = PR - PA, QR - QA
        c["zp"].wait_recv()
        c["pr"] = rsend(ref, x, oz, 0, PR, rtdev)
        c["pl"] = rsend(ref, x, oz, 0, PR, ldev)
        c["r"].wait_recv()
        c["fqr"] = rsend(ref, xl, z, PR + QA, QB, rtdev)
        c["zql"] = rsend(ref, xl, z, PR, QR, zdev)
        c["fpr"] = rsend(ref, xl, z, 0, PA, rtdev)
        c["l"].wait_recv()
        c["fql"] = rsend(ref, xr, z, PR, QA, ldev)
        c["zqr"] = rsend(ref, xr, z, PR, QR, zdev)
        c["fpl"] = rsend(ref, xr, z, PA, PB, ldev)

    def row_late(ref, c, split):
        PR, QR, PA, QA = split
        PB, QB = PR - PA, QR - QA
        c["pr"].wait_recv()
        c["gpr"] = rsend(ref, xl, oz, 0, PA, rtdev)
        c["pl"].wait_recv()
        c["gpl"] = rsend(ref, xr, oz, PA, PB, ldev)
        c["fqr"].wait_recv()
        c["zfr"] = rsend(ref, xf, z, PR + QA, QB, zdev)
        c["fql"].wait_recv()
        c["zfl"] = rsend(ref, xf, z, PR, QA, zdev)

    def sent(copies):
        for copy in copies:
            copy.wait_send()
            pending[:] = [other for other in pending if other is not copy]

    def row_end(c, names):
        for name in names:
            c[name].wait_recv()

    og = col_own(og_all)
    g_load.wait()
    gc = row_own(g_all, SPLIT_G)
    u_load.wait()
    uc = row_own(u_all, SPLIT_U)
    col_mid(og_all, og)
    col_late(og_all, og)
    dequantize(act_q, act_scale, in_all)
    inp = col_own(in_all)
    col_end(og)
    dw_load.wait()

    @pl.loop(0, FB // 256)
    def _(j):
        cols = pl.ds(pl.multiple_of(j * 256, 256), 256)
        part[:, cols] = nt(og_all[...], dw[cols, :]).astype(BF16)

    def prow(xx, zz, off):
        return (xx * 2 + zz) * 128 + off

    slot = [0]

    def psend(xx, zz, off, n, dev):
        at = slot[0]
        slot[0] += n
        return send(rows(part, prow(xx, zz, off), n), landed.at[pl.ds(at, n), :], dev), at

    def add(xx, zz, off, at, n):
        @pl.loop(0, n // 16)
        def _(i):
            here = pl.ds(pl.multiple_of(prow(xx, zz, off) + i * 16, 16), 16)
            there = pl.ds(pl.multiple_of(at + i * 16, 16), 16)
            part[here, :] = (part[here, :].astype(F32) + landed[there, :].astype(F32)).astype(BF16)

    order = (xf, xl, xr, x)
    zs = [psend(xx, oz, PR, QR, zdev) for xx in order]
    far_r = [psend(xf, zz, 0, PA, rtdev) for zz in (oz, z)]
    far_l = [psend(xf, zz, PA, PB, ldev) for zz in (oz, z)]
    row_mid(g_all, gc, SPLIT_G)
    for (copy, at), xx in zip(zs, order):
        copy.wait_recv()
        add(xx, z, PR, at, QR)
        if xx is xf:
            far_rq = psend(xf, z, PR + QA, QB, rtdev)
            far_lq = psend(xf, z, PR, QA, ldev)
    for (copy, at), zz in zip(far_r, (oz, z)):
        copy.wait_recv()
        add(xr, zz, 0, at, PA)
    nb_r = [psend(xr, oz, 0, PR, rtdev)]
    for (copy, at), zz in zip(far_l, (oz, z)):
        copy.wait_recv()
        add(xl, zz, PA, at, PB)
    nb_l = [psend(xl, oz, 0, PR, ldev)]
    far_rq[0].wait_recv()
    add(xr, z, PR + QA, far_rq[1], QB)
    nb_r.append(psend(xr, z, 0, 128, rtdev))
    far_lq[0].wait_recv()
    add(xl, z, PR, far_lq[1], QA)
    nb_l.append(psend(xl, z, 0, 128, ldev))

    row_mid(u_all, uc, SPLIT_U)
    row_late(g_all, gc, SPLIT_G)
    col_mid(in_all, inp)
    col_late(in_all, inp)

    nb_r[0][0].wait_recv()
    nb_l[0][0].wait_recv()
    add(x, oz, 0, nb_r[0][1], PR)
    add(x, oz, 0, nb_l[0][1], PR)
    last = psend(x, oz, 0, PR, zdev)
    row_late(u_all, uc, SPLIT_U)
    nb_r[1][0].wait_recv()
    nb_l[1][0].wait_recv()
    last[0].wait_recv()

    def own(lo, hi, landings):
        @pl.loop(lo // 16, hi // 16)
        def _(i):
            here = pl.ds(pl.multiple_of(row * 128 + i * 16, 16), 16)
            total = part[here, :].astype(F32)
            for at in landings:
                total = total + landed[pl.ds(pl.multiple_of(at + i * 16, 16), 16), :].astype(F32)
            h_all[here, :] = total.astype(BF16)

    own(0, PR, (nb_r[1][1], nb_l[1][1], last[1]))
    own(PR, 128, (nb_r[1][1], nb_l[1][1]))

    hc = row_own(h_all, SPLIT_H)

    col_end(inp)
    row_end(gc, ("zq", "zql", "zqr", "fpr", "fpl", "gpr", "gpl", "zfr", "zfl"))
    row_end(uc, ("zq", "zql", "zqr", "fpr", "fpl", "gpr", "gpl", "zfr", "zfl"))

    @pl.loop(0, T // 16)
    def _(i):
        here = pl.ds(pl.multiple_of(i * 16, 16), 16)
        for j in range(FB // 256):
            cols = pl.ds(j * 256, 256)
            gv = g_all[here, cols].astype(F32)
            hid[here, cols] = (gv * jax.nn.sigmoid(gv) * u_all[here, cols].astype(F32)).astype(BF16)

    @pl.loop(0, FB // 256)
    def _(j):
        cols = pl.ds(pl.multiple_of(j * 256, 256), 256)
        dw[cols, :] = (tn(hid[:, cols], og_all[...]) * FACTOR).astype(BF16)


    places = [(xl, z), (xr, z), (x, z), (x, oz), (xl, oz), (xr, oz), (xf, z), (xf, oz)]
    for pos, (xx, zz) in enumerate(places):
        in_t[:, pos * 128 : pos * 128 + 128] = in_all[pl.ds(pl.multiple_of((xx * 2 + zz) * 128, 128), 128), :].T

    def pointwise(at, to):
        @pl.loop(0, 8)
        def _(i):
            here = pl.ds(pl.multiple_of(at + i * 16, 16), 16)
            there = pl.ds(pl.multiple_of(to + i * 16, 16), 16)
            for j in range(FB // 256):
                cols = pl.ds(j * 256, 256)
                gv = g_all[here, cols].astype(F32)
                hv = h_all[here, cols].astype(F32)
                s = jax.nn.sigmoid(gv)
                gd[there, cols] = (hv * u_all[here, cols].astype(F32) * s * (1.0 + gv * (1.0 - s))).astype(BF16)
                ud[there, cols] = (hv * gv * s).astype(BF16)

    def weight_grad(delta, total, quarter):
        here = pl.ds(quarter * 256, 256)
        total[here, :] = (jnp.dot(in_t[here, :], delta[...], preferred_element_type=F32) * FACTOR).astype(BF16)

    def block(pos):
        xx, zz = places[pos]
        at = xx * 2 + zz
        return pos, at, lax.rem(at, 4), lax.div(at, 4)

    def group(blocks):
        here = pl.ds(blocks[0][0] * 128, 128 * len(blocks))
        for pos, at, _, _ in blocks:
            pointwise(at * 128, pos * 128)

        @pl.loop(0, DB // 256)
        def _(j):
            cols = pl.ds(pl.multiple_of(j * 256, 256), 256)
            act_part[here, cols] = (nt(gd[here, :], gw[cols, :]) + nt(ud[here, :], uw[cols, :])).astype(BF16)

        return [send(rows(act_part, pos * 128 + ocore * 64, 64), sib_in.at[pos], sdev) for pos, _, _, _ in blocks]

    LO, HI = pl.ds(0, 32), pl.ds(32, 32)

    def reduce_y(blocks, sib):
        result = []
        for (i, _, yd, _), copy in zip(blocks, sib):
            copy.wait_recv()
            mine = act_part[pl.ds(pl.multiple_of(i * 128 + core * 64, 64), 64), :]
            y_out[i] = (mine.astype(F32) + sib_in[i].astype(F32)).astype(BF16)
            where = lax.rem(y + 4 - yd, 4)

            def half(src, dst, dev):
                return make(y_out.at[i, src, :], dst.at[src, :], dev)

            c = dict(
                where=where,
                far_lo=half(LO, y_far.at[i], yldev),
                far_hi=half(HI, y_far.at[i], yrdev),
                l_hi=half(HI, y_in.at[i, 0], yldev),
                l_lo=half(LO, y_in.at[i, 0], yldev),
                r_lo=half(LO, y_in.at[i, 1], yrdev),
                r_hi=half(HI, y_in.at[i, 1], yrdev),
            )

            @pl.when(where == 2)
            def _():
                c["far_lo"].start()
                c["far_hi"].start()

            @pl.when(where == 1)
            def _():
                c["l_hi"].start()

            @pl.when(where == 3)
            def _():
                c["r_lo"].start()

            result.append(c)
        return result

    def relay(blocks, copies):
        for (i, _, _, _), c in zip(blocks, copies):
            for at, part_of, far, on in ((1, LO, "far_lo", "l_lo"), (3, HI, "far_hi", "r_hi")):

                @pl.when(c["where"] == at)
                def _():
                    c[far].wait_recv()
                    y_out[i, part_of, :] = (
                        y_out[i, part_of, :].astype(F32) + y_far[i, part_of, :].astype(F32)
                    ).astype(BF16)
                    c[on].start()

    def reduce_end(blocks, copies, zcopy):
        for (i, _, _, zd), c in zip(blocks, copies):

            @pl.when(c["where"] == 0)
            def _():
                for name in ("l_hi", "r_lo", "l_lo", "r_hi"):
                    c[name].wait_recv()
                total = y_out[i].astype(F32) + y_in[i, 0].astype(F32) + y_in[i, 1].astype(F32)

                @pl.when(zd == zh)
                def _():
                    final[...] = total

                @pl.when(zd != zh)
                def _():
                    z_out[...] = total.astype(BF16)
                    zcopy.start()

            for at, names in ((2, ("far_lo", "far_hi")), (1, ("l_hi", "l_lo")), (3, ("r_lo", "r_hi"))):

                @pl.when(c["where"] == at)
                def _():
                    for name in names:
                        c[name].wait_send()

    gw_load.wait()
    uw_load.wait()
    zcopy = make(z_out, z_in, hdev)

    row_mid(h_all, hc, SPLIT_H)
    work = [[block(0), block(1)], [block(2), block(3)], [block(4), block(5)], [block(6)], [block(7)]]
    s0 = group(work[0])
    row_end(hc, ("zq",))
    s1 = group(work[1])
    row_late(h_all, hc, SPLIT_H)
    y0 = reduce_y(work[0], s0)
    y1 = reduce_y(work[1], s1)
    row_end(hc, ("zql", "zqr"))
    s2 = group(work[2])
    relay(work[0], y0)
    relay(work[1], y1)
    row_end(hc, ("fpr", "fpl"))
    s3 = group(work[3])
    y2 = reduce_y(work[2], s2)
    reduce_end(work[0], y0, zcopy)
    reduce_end(work[1], y1, zcopy)
    row_end(hc, ("gpr", "gpl", "zfr", "zfl"))
    s4 = group(work[4])
    y3 = reduce_y(work[3], s3)
    relay(work[2], y2)
    sent([copy for copy, _ in zs + far_r + far_l + nb_r + nb_l + [far_rq, far_lq, last]])
    y4 = reduce_y(work[4], s4)
    weight_grad(gd, part, 0)
    relay(work[3], y3)
    weight_grad(gd, part, 1)
    relay(work[4], y4)
    reduce_end(work[2], y2, zcopy)
    weight_grad(gd, part, 2)
    reduce_end(work[3], y3, zcopy)
    weight_grad(gd, part, 3)
    reduce_end(work[4], y4, zcopy)
    sent(list(gc.values()))
    for quarter in range(4):
        weight_grad(ud, g_all, quarter)
    zcopy.wait()
    act_grad[...] = (final[...] + z_in[...].astype(F32)).astype(BF16)
    for copy in pending:
        copy.wait_send()
    assert count[0] == N_SEMS, count[0]


def exchange(*args):
    any_spec = pl.BlockSpec(memory_space=pl.ANY)
    vmem = pl.BlockSpec(memory_space=pltpu.VMEM)
    wide = pltpu.VMEM((T, FB), BF16)
    return pl.pallas_call(
        kernel,
        out_shape=(
            pltpu.VMEM((64, DB), BF16),
            pltpu.VMEM((DB, FB), BF16),
            pltpu.VMEM((FB, DB), BF16),
            pltpu.VMEM((DB, FB), BF16),
        ),
        in_specs=[vmem] * 4 + [any_spec] * 5,
        out_specs=(vmem,) * 4,
        scratch_shapes=[
            wide, wide,
            pltpu.VMEM((4 * QR + 2 * PR + QR + 2 * (128 + PR) + PR, FB), BF16),
            pltpu.VMEM((T, DB), BF16),
            pltpu.VMEM((T, DB), BF16),
            pltpu.VMEM((DB, FB), BF16),
            pltpu.VMEM((DB, FB), BF16),
            wide, wide, wide,
            pltpu.VMEM((DB, T), BF16),
            pltpu.VMEM((T, DB), BF16),
            pltpu.VMEM((8, 64, DB), BF16),
            pltpu.VMEM((8, 64, DB), BF16),
            pltpu.VMEM((8, 64, DB), BF16),
            pltpu.VMEM((8, 2, 64, DB), BF16),
            pltpu.VMEM((64, DB), BF16),
            pltpu.VMEM((64, DB), BF16),
            pltpu.VMEM((64, DB), F32),
            pltpu.SemaphoreType.DMA((N_SEMS,)),
            pltpu.SemaphoreType.DMA((N_SEMS,)),
            pltpu.SemaphoreType.DMA((32,)),
        ],
        compiler_params=pltpu.CompilerParams(
            collective_id=0, has_side_effects=True, vmem_limit_bytes=LIMIT * 2**20
        ),
        name="exchange",
    )(*args)


def finish_kernel(*refs):
    copies = [pltpu.make_async_copy(refs[i], refs[4 + i], refs[8].at[i]) for i in range(4)]
    for copy in copies:
        copy.start()
    for copy in copies:
        copy.wait()


def finish(*arrays):
    return pl.pallas_call(
        finish_kernel,
        out_shape=tuple(jax.ShapeDtypeStruct(a.shape, BF16) for a in arrays),
        in_specs=[pl.BlockSpec(memory_space=pltpu.VMEM)] * 4,
        out_specs=(pl.BlockSpec(memory_space=pl.ANY),) * 4,
        scratch_shapes=[pltpu.SemaphoreType.DMA((4,))],
        compiler_params=pltpu.CompilerParams(vmem_limit_bytes=24 * 2**20),
        name="finish",
    )(*arrays)


def shards(act_q, act_scale, grad_q, grad_scale, *args):
    act, gate, down, up = exchange(act_q, act_scale.T, grad_q, grad_scale.T, *args)
    return finish(act, gate, up, down)


def solution(mesh):
    rc, cr = P("row", "col"), P("col", "row")
    return jax.shard_map(
        shards,
        mesh=mesh,
        in_specs=(cr, cr, cr, cr, rc, rc, rc, rc, cr),
        out_specs=(cr, rc, rc, cr),
        check_vma=False,
    )
```
